32 devices in a mesh: st: 4 (over y, core), col: 8 (over z, x).
Axes of the slice: x: 2, y: 2, z: 4, core: 2. Of those that a mesh axis runs over, the one named last changes fastest.
Arguments:
- forcing: bfloat16 [8, 2048, 2048], P('st', None, 'col'), may hold values from -6 to 6
- operator_rows: bfloat16 [8, 2048, 2048], P('st', 'col'), may hold values from -0.078125 to 0.078125
- counts: int32 [8], P('st'), may hold values from 1 to 3, as said below
- owner_map: int32 [8, 8], P('st'), may hold values from 0 to 7, each once within a row
Outputs:
- adjoint: bfloat16 [8, 2048, 2048], P('st', None, 'col')
The draws below stay inside these ranges and needn't reach their ends.
Inputs may be any that keep to these rules, and one draw needn't show every extreme that they name: `counts`: some station has exactly 3 terms. `owner_map`: each station's row is a permutation of the row blocks.
All inputs are finite; a program needn't handle non-finite values.
Results may differ from the reference program's by a relative error of at most 0.015.
Values may be sent and summed in bfloat16 or wider, within the bound.
A program may use at most 128 MiB of HBM per device.

```python
import jax
import jax.numpy as jnp
from jax import lax

N = 2048
KMAX = 3
STATIONS = 8
COLS = 2048
OWNERS = 8


def draw_counts(key, part):
    first_key, second_key = jax.random.split(jax.random.fold_in(key, 11))
    base = jax.random.randint(first_key, (STATIONS,), 1, KMAX + 1)
    spot = jax.random.randint(second_key, (), 0, STATIONS)
    return jnp.where(jnp.arange(STATIONS) == spot, KMAX, base).astype(jnp.int32)


def shard_levels(stream_key, shape, cuts, least, largest):
    gain = 1.0
    for position, shards_of in cuts:
        steps = jax.random.uniform(jax.random.fold_in(jax.random.fold_in(stream_key, 6), position), (shards_of,), jnp.float32, least / len(cuts), largest / len(cuts))
        gain = gain * jnp.repeat(jnp.exp(steps), shape[position] // shards_of).reshape((-1,) + (1,) * (len(shape) - 1 - position))
    return gain


def scatter_about(stream_key, dims, width, most, cuts=(), held_as=jnp.bfloat16):
    array = jax.random.normal(stream_key, dims, jnp.float32) * width
    if len(cuts) > 0:
        array = shard_levels(stream_key, dims, cuts, -0.22, 0.18) * array
    return jnp.clip(array, min=-most, max=most).astype(held_as)


def setup_inputs(seed: int = 0) -> dict:
    arg_keys = jax.random.split(jax.random.key(seed), 5)
    forcing = scatter_about(arg_keys[0], (STATIONS, N, COLS), 1.0, 6.0, ((0, 4), (2, 8)))
    operator_rows = scatter_about(arg_keys[1], (STATIONS, N, N), (3 * N) ** -0.5, 0.078125, ((0, 4), (1, 8)))
    counts = draw_counts(jax.random.fold_in(arg_keys[4], 71), 0)
    owner_map = jax.vmap(lambda own: jax.random.permutation(own, OWNERS))(jax.random.split(arg_keys[3], STATIONS)).reshape((STATIONS, OWNERS)).astype(jnp.int32)
    return dict(forcing=forcing, operator_rows=operator_rows, counts=counts, owner_map=owner_map)


def reorder(stored, mapping):
    owners = mapping.shape[0]
    blocks = stored.reshape(owners, stored.shape[0] // owners, stored.shape[1])
    slots = jnp.arange(owners, dtype=jnp.int32)
    inverse = jnp.sum(jnp.where(mapping[None, :] == slots[:, None], slots[None, :], 0), axis=1).astype(jnp.int32)
    return jnp.take(blocks, inverse, axis=0).reshape(stored.shape)


def advance(matrix, incoming, force, count):
    start = (incoming.astype(jnp.float32) + force.astype(jnp.float32)).astype(jnp.bfloat16)

    def power(index, carry):
        phi, total = carry
        phi = jnp.dot(matrix, phi, preferred_element_type=jnp.float32).astype(jnp.bfloat16)
        return phi, total + phi.astype(jnp.float32)

    phi, total = lax.fori_loop(0, count, power, (start, start.astype(jnp.float32)))
    return (0.7 * total).astype(jnp.bfloat16)


def reference(forcing, operator_rows, counts, owner_map):
    def station(carry, items):
        force, stored, count, mapping = items
        matrix = reorder(stored, mapping)
        state = advance(matrix, carry, force, count)
        return state, state

    initial = jnp.zeros((N, COLS), jnp.bfloat16)
    last, states = lax.scan(station, initial, (forcing, operator_rows, counts, owner_map), reverse=True)
    return states
```

```python
import functools

import jax
import jax.numpy as jnp
from jax import lax
from jax.experimental import pallas as pl
from jax.experimental.pallas import tpu as pltpu
from jax.sharding import PartitionSpec as P

MESH = pl.DeviceIdType.MESH


def ring_index(pos, n):
    if n % 2:
        return pos
    return jnp.where(pos < n // 2, 2 * pos, 2 * (n - 1 - pos) + 1)


def ring_position(index, n):
    if n % 2:
        return index
    return jnp.where(index % 2 == 0, index // 2, n - 1 - index // 2)


def gather_kernel(n, rows_ref, out_ref, local_sem, send_sem, recv_sem):
    stations, block = rows_ref.shape[0], rows_ref.shape[1]
    half = block // 2
    me = lax.axis_index("col")
    pos = ring_position(me, n)
    right = ring_index((pos + 1) % n, n)
    left = ring_index((pos + n - 1) % n, n)
    peers = (right, left)

    barrier = pltpu.get_barrier_semaphore()
    for peer in peers:
        pl.semaphore_signal(barrier, inc=1, device_id={"col": peer}, device_id_type=MESH)
    pl.semaphore_wait(barrier, 2)

    own = [pltpu.make_async_copy(rows_ref.at[j], out_ref.at[j, me], local_sem.at[j]) for j in range(stations)]
    for copy in own:
        copy.start()

    def part(d):
        return pl.ds(d * half, half)

    def copy_of(j, d, t):
        slot = ring_index((pos - t + n) % n if d == 0 else (pos + t) % n, n)
        source = rows_ref.at[j, part(d)] if t == 0 else out_ref.at[j, slot, part(d)]
        return pltpu.make_async_remote_copy(
            src_ref=source,
            dst_ref=out_ref.at[j, slot, part(d)],
            send_sem=send_sem.at[j, d, t],
            recv_sem=recv_sem.at[j, d, t],
            device_id={"col": peers[d]},
            device_id_type=MESH,
        )

    flows = [(j, d) for j in reversed(range(stations)) for d in range(2)]
    copies = {}
    for t in range(n - 1):
        for j, d in flows:
            if t > 0:
                copies[j, d, t - 1].wait_recv()
            copies[j, d, t] = copy_of(j, d, t)
            copies[j, d, t].start()
    for j, d in flows:
        copies[j, d, n - 2].wait_recv()
    for copy in copies.values():
        copy.wait_send()
    for copy in own:
        copy.wait()


def gather(rows, n):
    stations, block, width = rows.shape
    return pl.pallas_call(
        functools.partial(gather_kernel, n),
        out_shape=jax.ShapeDtypeStruct((stations, n, block, width), rows.dtype),
        in_specs=[pl.BlockSpec(memory_space=pl.ANY)],
        out_specs=pl.BlockSpec(memory_space=pl.ANY),
        scratch_shapes=[
            pltpu.SemaphoreType.DMA((stations,)),
            pltpu.SemaphoreType.DMA((stations, 2, n - 1)),
            pltpu.SemaphoreType.DMA((stations, 2, n - 1)),
        ],
        compiler_params=pltpu.CompilerParams(collective_id=0, has_side_effects=True),
        name="gather_operators",
    )(rows)


def march_kernel(tile, counts_ref, slots_ref, blocks_ref, incoming_ref, force_ref, out_ref, last_ref, matrix, phis, total, sem):
    stations, n, block, size = blocks_ref.shape
    order = list(reversed(range(stations)))

    def fetch(j, b):
        return pltpu.make_async_copy(blocks_ref.at[j, slots_ref[j, b]], matrix.at[j, pl.ds(b * block, block)], sem.at[j, b])

    for j in order:
        for b in range(n):
            fetch(j, b).start()

    tiles = size // tile
    for j in order:
        before = incoming_ref[...] if j == order[0] else out_ref[j + 1]
        start = (before.astype(jnp.float32) + force_ref[j].astype(jnp.float32)).astype(jnp.bfloat16)
        phis[0] = start
        total[...] = start.astype(jnp.float32)
        for b in range(n):
            fetch(j, b).wait()

        def power(k, _):
            now, later = lax.rem(k, 2), lax.rem(k + 1, 2)

            def rows(i, _):
                at = pl.ds(pl.multiple_of(i * tile, tile), tile)
                phi = jnp.dot(matrix[j, at, :], phis[now], preferred_element_type=jnp.float32).astype(jnp.bfloat16)
                phis[later, at, :] = phi
                total[at, :] += phi.astype(jnp.float32)
                return 0

            return lax.fori_loop(0, tiles, rows, 0)

        lax.fori_loop(0, counts_ref[j], power, 0)
        out_ref[j] = (0.7 * total[...]).astype(jnp.bfloat16)
    last_ref[...] = out_ref[order[-1]]


def march(counts, slots, blocks, incoming, force):
    stations, n, block, size = blocks.shape
    width = force.shape[2]
    vmem = pl.BlockSpec(memory_space=pltpu.VMEM)
    smem = pl.BlockSpec(memory_space=pltpu.SMEM)
    tile = 512 if size % 512 == 0 else size
    return pl.pallas_call(
        functools.partial(march_kernel, tile),
        out_shape=(jax.ShapeDtypeStruct(force.shape, jnp.bfloat16), jax.ShapeDtypeStruct(incoming.shape, jnp.bfloat16)),
        in_specs=[smem, smem, pl.BlockSpec(memory_space=pl.ANY), vmem, vmem],
        out_specs=(vmem, vmem),
        scratch_shapes=[
            pltpu.VMEM((stations, size, size), jnp.bfloat16),
            pltpu.VMEM((2, size, width), jnp.bfloat16),
            pltpu.VMEM((size, width), jnp.float32),
            pltpu.SemaphoreType.DMA((stations, n)),
        ],
        compiler_params=pltpu.CompilerParams(vmem_limit_bytes=48 * 1024 * 1024),
        name="march_stations",
    )(counts, slots, blocks, incoming, force)


def shards(forcing, operator_rows, counts, owner_map):
    n = lax.axis_size("col")
    sections = lax.axis_size("st")
    place = lax.axis_index("st")
    blocks = gather(operator_rows, n)
    ids = jnp.arange(n, dtype=jnp.int32)
    slots = jnp.sum(jnp.where(owner_map[:, None, :] == ids[None, :, None], ids[None, None, :], 0), axis=2).astype(jnp.int32)
    outgoing = jnp.zeros(forcing.shape[1:], jnp.bfloat16)
    result = jnp.zeros_like(forcing)
    for turn in range(sections):
        source = sections - turn
        received = outgoing if turn == 0 else lax.ppermute(outgoing, "st", [(source, source - 1)])

        def work(operands):
            state, _ = operands
            made, last = march(counts, slots, blocks, state, forcing)
            return last, made

        outgoing, result = lax.cond(place == sections - 1 - turn, work, lambda operands: operands, (received, result))
    return result


def solution(mesh):
    in_specs = (P("st", None, "col"), P("st", "col", None), P("st"), P("st", None))
    out_specs = P("st", None, "col")
    return jax.shard_map(shards, mesh=mesh, in_specs=in_specs, out_specs=out_specs, check_vma=False)
```

```python
import functools

import jax
import jax.numpy as jnp
from jax import lax
from jax.experimental import pallas as pl
from jax.experimental.pallas import tpu as pltpu
from jax.sharding import PartitionSpec as P

MESH = pl.DeviceIdType.MESH
TERMS = 3


def ring_index(pos, n):
    if n % 2:
        return pos
    return jnp.where(pos < n // 2, 2 * pos, 2 * (n - 1 - pos) + 1)


def ring_position(index, n):
    if n % 2:
        return index
    return jnp.where(index % 2 == 0, index // 2, n - 1 - index // 2)


def kernel(n, sections, counts_ref, slots_ref, rows_ref, force_ref, out_ref, matrix, phi, stage, total, incoming,
           local_sem, send_sem, recv_sem, turn_sem, state_send, state_recv):
    stations, block, size = rows_ref.shape
    half = block // 2
    me, place = lax.axis_index("col"), lax.axis_index("st")
    pos = ring_position(me, n)
    peers = (ring_index((pos + 1) % n, n), ring_index((pos + n - 1) % n, n))
    top = sections - 1

    barrier = pltpu.get_barrier_semaphore()
    for peer in peers:
        pl.semaphore_signal(barrier, inc=1, device_id={"col": peer}, device_id_type=MESH)

    @pl.when(place > 0)
    def _():
        pl.semaphore_signal(barrier, inc=1, device_id={"st": place - 1}, device_id_type=MESH)

    @pl.when(place < top)
    def _():
        pl.semaphore_signal(barrier, inc=1, device_id={"st": place + 1}, device_id_type=MESH)

    pl.semaphore_wait(barrier, 2 + jnp.where(place > 0, 1, 0) + jnp.where(place < top, 1, 0))

    own = [pltpu.make_async_copy(rows_ref.at[j], matrix.at[j, me], local_sem.at[j]) for j in range(stations)]
    for copy in own:
        copy.start()

    if sections > 1:
        @pl.when(place == top - 1)
        def _():
            pl.semaphore_wait(turn_sem, 1)

    def copy_of(j, d, t):
        slot = ring_index((pos - t + n) % n if d == 0 else (pos + t) % n, n)
        part = pl.ds(d * half, half)
        return pltpu.make_async_remote_copy(
            src_ref=rows_ref.at[j, part] if t == 0 else matrix.at[j, slot, part],
            dst_ref=matrix.at[j, slot, part],
            send_sem=send_sem.at[j, d, t],
            recv_sem=recv_sem.at[j, d, t],
            device_id={"col": peers[d]},
            device_id_type=MESH,
        )

    order = list(reversed(range(stations)))
    flows = [(j, d) for j in order for d in range(2)]
    copies = {}
    for t in range(n - 1):
        for j, d in flows:
            if t > 0:
                copies[j, d, t - 1].wait_recv()
            copies[j, d, t] = copy_of(j, d, t)
            copies[j, d, t].start()

    if sections > 1:
        @pl.when(place == top)
        def _():
            pl.semaphore_signal(turn_sem, inc=1, device_id={"st": place - 1}, device_id_type=MESH)

    for j, d in flows:
        copies[j, d, n - 2].wait_recv()
    for copy in copies.values():
        copy.wait_send()
    for copy in own:
        copy.wait()

    handoff = pltpu.make_async_remote_copy(
        src_ref=out_ref.at[order[-1]],
        dst_ref=incoming,
        send_sem=state_send,
        recv_sem=state_recv,
        device_id={"st": jnp.maximum(place - 1, 0)},
        device_id_type=MESH,
    )

    @pl.when(place == top)
    def _():
        incoming[...] = jnp.zeros_like(incoming)

    @pl.when(place < top)
    def _():
        handoff.wait_recv()

    group = max(1, min(n, 512 // block))
    while n % group:
        group -= 1
    for j in order:
        before = incoming if j == order[0] else out_ref.at[j + 1]

        def begin(b, _):
            at = pl.ds(pl.multiple_of(b * block, block), block)
            start = (before[at, :].astype(jnp.float32) + force_ref[j, at, :].astype(jnp.float32)).astype(jnp.bfloat16)
            phi[at, :] = start
            total[at, :] = start.astype(jnp.float32)
            return 0

        lax.fori_loop(0, n, begin, 0)

        def power(k, _):
            def product(i, _):
                at = pl.ds(i * group, group)
                rows = matrix[j, at].reshape(group * block, size)
                made = jnp.dot(rows, phi[...], preferred_element_type=jnp.float32).astype(jnp.bfloat16)
                stage[at] = made.reshape(group, block, made.shape[1])
                return 0

            lax.fori_loop(0, n // group, product, 0)
            counted = jnp.full((block, phi.shape[1]), counts_ref[j], jnp.int32) > k

            def settle(b, _):
                at = pl.ds(pl.multiple_of(b * block, block), block)
                piece = stage[slots_ref[j, b]]
                phi[at, :] = piece
                total[at, :] += jnp.where(counted, piece.astype(jnp.float32), 0.0)
                return 0

            lax.fori_loop(0, n, settle, 0)
            return 0

        lax.fori_loop(0, TERMS, power, 0)
        out_ref[j] = (0.7 * total[...]).astype(jnp.bfloat16)

    @pl.when(place > 0)
    def _():
        handoff.start()
        handoff.wait_send()


def shards(forcing, operator_rows, counts, owner_map):
    n = lax.axis_size("col")
    sections = lax.axis_size("st")
    ids = jnp.arange(n, dtype=jnp.int32)
    slots = jnp.sum(jnp.where(owner_map[:, None, :] == ids[None, :, None], ids[None, None, :], 0), axis=2).astype(jnp.int32)
    stations, block, size = operator_rows.shape
    width = forcing.shape[2]
    vmem = pl.BlockSpec(memory_space=pltpu.VMEM)
    smem = pl.BlockSpec(memory_space=pltpu.SMEM)
    return pl.pallas_call(
        functools.partial(kernel, n, sections),
        out_shape=jax.ShapeDtypeStruct(forcing.shape, forcing.dtype),
        in_specs=[smem, smem, pl.BlockSpec(memory_space=pl.ANY), vmem],
        out_specs=vmem,
        scratch_shapes=[
            pltpu.VMEM((stations, n, block, size), jnp.bfloat16),
            pltpu.VMEM((size, width), jnp.bfloat16),
            pltpu.VMEM((n, block, width), jnp.bfloat16),
            pltpu.VMEM((size, width), jnp.float32),
            pltpu.VMEM((size, width), jnp.bfloat16),
            pltpu.SemaphoreType.DMA((stations,)),
            pltpu.SemaphoreType.DMA((stations, 2, n - 1)),
            pltpu.SemaphoreType.DMA((stations, 2, n - 1)),
            pltpu.SemaphoreType.REGULAR,
            pltpu.SemaphoreType.DMA,
            pltpu.SemaphoreType.DMA,
        ],
        compiler_params=pltpu.CompilerParams(collective_id=0, has_side_effects=True, vmem_limit_bytes=48 * 1024 * 1024),
        name="gather_and_march",
    )(counts, slots, operator_rows, forcing)


def solution(mesh):
    in_specs = (P("st", None, "col"), P("st", "col", None), P("st"), P("st", None))
    out_specs = P("st", None, "col")
    return jax.shard_map(shards, mesh=mesh, in_specs=in_specs, out_specs=out_specs, check_vma=False)
```

```python
import functools

import jax
import jax.numpy as jnp
from jax import lax
from jax.experimental import pallas as pl
from jax.experimental.pallas import tpu as pltpu
from jax.sharding import PartitionSpec as P

MESH = pl.DeviceIdType.MESH
TERMS = 3
PIECES = 1


def ring_index(pos, n):
    if n % 2:
        return pos
    return jnp.where(pos < n // 2, 2 * pos, 2 * (n - 1 - pos) + 1)


def ring_position(index, n):
    if n % 2:
        return index
    return jnp.where(index % 2 == 0, index // 2, n - 1 - index // 2)


def kernel(n, sections, counts_ref, slots_ref, rows_ref, force_ref, out_ref, matrix, phis, incoming,
           local_sem, send_sem, recv_sem, turn_sem, state_send, state_recv):
    stations, block, size = rows_ref.shape
    half = block // 2
    me, place = lax.axis_index("col"), lax.axis_index("st")
    pos = ring_position(me, n)
    peers = (ring_index((pos + 1) % n, n), ring_index((pos + n - 1) % n, n))
    top = sections - 1

    barrier = pltpu.get_barrier_semaphore()
    for peer in peers:
        pl.semaphore_signal(barrier, inc=1, device_id={"col": peer}, device_id_type=MESH)

    @pl.when(place > 0)
    def _():
        pl.semaphore_signal(barrier, inc=1, device_id={"st": place - 1}, device_id_type=MESH)

    @pl.when(place < top)
    def _():
        pl.semaphore_signal(barrier, inc=1, device_id={"st": place + 1}, device_id_type=MESH)

    pl.semaphore_wait(barrier, 2 + jnp.where(place > 0, 1, 0) + jnp.where(place < top, 1, 0))

    own = [pltpu.make_async_copy(rows_ref.at[j], matrix.at[j, me], local_sem.at[j]) for j in range(stations)]
    for copy in own:
        copy.start()

    if sections > 1:
        @pl.when(place == top - 1)
        def _():
            pl.semaphore_wait(turn_sem, 1)

    def copy_of(j, d, t):
        slot = ring_index((pos - t + n) % n if d == 0 else (pos + t) % n, n)
        part = pl.ds(d * half, half)
        return pltpu.make_async_remote_copy(
            src_ref=rows_ref.at[j, part] if t == 0 else matrix.at[j, slot, part],
            dst_ref=matrix.at[j, slot, part],
            send_sem=send_sem.at[j, d, t],
            recv_sem=recv_sem.at[j, d, t],
            device_id={"col": peers[d]},
            device_id_type=MESH,
        )

    order = list(reversed(range(stations)))
    flows = [(j, d) for j in order for d in range(2)]
    copies = {}
    for t in range(n - 1):
        for j, d in flows:
            if t > 0:
                copies[j, d, t - 1].wait_recv()
            copies[j, d, t] = copy_of(j, d, t)
            copies[j, d, t].start()

    if sections > 1:
        @pl.when(place == top)
        def _():
            pl.semaphore_signal(turn_sem, inc=1, device_id={"st": place - 1}, device_id_type=MESH)

    for j, d in flows:
        copies[j, d, n - 2].wait_recv()
    for copy in copies.values():
        copy.wait_send()
    for copy in own:
        copy.wait()

    pieces = PIECES if size % (PIECES * 16) == 0 and n % PIECES == 0 else 1
    span = size // pieces

    def handoff(i):
        return pltpu.make_async_remote_copy(
            src_ref=out_ref.at[order[-1], pl.ds(i * span, span)],
            dst_ref=incoming.at[pl.ds(i * span, span)],
            send_sem=state_send.at[i],
            recv_sem=state_recv.at[i],
            device_id={"st": jnp.maximum(place - 1, 0)},
            device_id_type=MESH,
        )

    @pl.when(place == top)
    def _():
        incoming[...] = jnp.zeros_like(incoming)

    def product(j, source, first, count):
        rows = jnp.concatenate([matrix[j, slots_ref[j, first + b]] for b in range(count)], axis=0)
        return jnp.dot(rows, source, preferred_element_type=jnp.float32).astype(jnp.bfloat16)

    for j in order:
        for i in range(pieces):
            at = pl.ds(i * span, span)
            if j == order[0]:
                @pl.when(place < top)
                def _():
                    handoff(i).wait_recv()
                before = incoming[at, :]
            else:
                before = out_ref[j + 1, at, :]
            phis[0, at, :] = (before.astype(jnp.float32) + force_ref[j, at, :].astype(jnp.float32)).astype(jnp.bfloat16)

        def power(k, _):
            phis[k + 1] = product(j, phis[k], 0, n)
            return 0

        lax.fori_loop(0, TERMS - 1, power, 0)
        for i in range(pieces):
            at = pl.ds(i * span, span)
            terms = [phis[k, at, :] for k in range(TERMS)]
            terms.append(product(j, phis[TERMS - 1], i * (n // pieces), n // pieces))
            total = terms[0].astype(jnp.float32)
            for k in range(1, TERMS + 1):
                counted = jnp.full(total.shape, counts_ref[j], jnp.int32) >= k
                total += jnp.where(counted, terms[k].astype(jnp.float32), 0.0)
            out_ref[j, at, :] = (0.7 * total).astype(jnp.bfloat16)
            if j == order[-1]:
                @pl.when(place > 0)
                def _():
                    handoff(i).start()

    @pl.when(place > 0)
    def _():
        for i in range(pieces):
            handoff(i).wait_send()


def shards(forcing, operator_rows, counts, owner_map):
    n = lax.axis_size("col")
    sections = lax.axis_size("st")
    ids = jnp.arange(n, dtype=jnp.int32)
    slots = jnp.sum(jnp.where(owner_map[:, None, :] == ids[None, :, None], ids[None, None, :], 0), axis=2).astype(jnp.int32)
    stations, block, size = operator_rows.shape
    width = forcing.shape[2]
    vmem = pl.BlockSpec(memory_space=pltpu.VMEM)
    smem = pl.BlockSpec(memory_space=pltpu.SMEM)
    return pl.pallas_call(
        functools.partial(kernel, n, sections),
        out_shape=jax.ShapeDtypeStruct(forcing.shape, forcing.dtype),
        in_specs=[smem, smem, pl.BlockSpec(memory_space=pl.ANY), vmem],
        out_specs=vmem,
        scratch_shapes=[
            pltpu.VMEM((stations, n, block, size), jnp.bfloat16),
            pltpu.VMEM((TERMS, size, width), jnp.bfloat16),
            pltpu.VMEM((size, width), jnp.bfloat16),
            pltpu.SemaphoreType.DMA((stations,)),
            pltpu.SemaphoreType.DMA((stations, 2, n - 1)),
            pltpu.SemaphoreType.DMA((stations, 2, n - 1)),
            pltpu.SemaphoreType.REGULAR,
            pltpu.SemaphoreType.DMA((PIECES,)),
            pltpu.SemaphoreType.DMA((PIECES,)),
        ],
        compiler_params=pltpu.CompilerParams(collective_id=0, has_side_effects=True, vmem_limit_bytes=48 * 1024 * 1024),
        name="gather_and_march",
    )(counts, slots, operator_rows, forcing)


def solution(mesh):
    in_specs = (P("st", None, "col"), P("st", "col", None), P("st"), P("st", None))
    out_specs = P("st", None, "col")
    return jax.shard_map(shards, mesh=mesh, in_specs=in_specs, out_specs=out_specs, check_vma=False)
```
